32 devices in a mesh: groups: 2 (over y), pts: 4 (over z), freq: 2 (over x), sub: 2 (over core).
Axes of the slice: x: 2, y: 2, z: 4, core: 2. Of those that a mesh axis runs over, the one named last changes fastest.
Arguments:
- series: bfloat16 [2048, 8, 16384], P(('pts', 'sub'), 'freq', 'groups'), parts along dimension 2, may hold values from -256 to 256, as said below
- block_start: int32 [15], replicated, may hold values from 0 to 1792, as said below
- freq_index: int32 [64], replicated, may hold values from 0 to 128, as said below
Outputs:
- modes: float32 [2, 64, 16, 8192], P(None, 'freq', 'groups', ('pts', 'sub')), parts along dimension 2
- spectrum: float32 [128], P(('groups', 'freq')), parts along dimension 0
The draws below stay inside these ranges and needn't reach their ends.
There are 2 independent parts, one for each index of `groups`. The reference program is written for one: setup_inputs(seed, part) draws one part's arguments, and reference() takes and returns one part's arrays. A program takes and returns all parts, laid end to end along the dimension named above; an argument that names none is the same for every part. Nothing has to cross between parts.
Inputs may be any that keep to these rules, and one draw needn't show every extreme that they name: series is finite. block_start rises with the block; its first entry is 0 and its last is 1792; every other entry lies within 32 of its block number times 128. freq_index holds 64 different bins, 0 and 128 among them.
All inputs are finite; a program needn't handle non-finite values.
Results may differ from the reference program's by a relative error of at most 0.0041.
Values may be sent and summed in bfloat16 or wider, within the bound.
A program may use at most 128 MiB of HBM per device.

```python
import math
import jax
import jax.numpy as jnp
from jax import lax

NFFT = 256
BLOCKS = 15
NF = 64
GX = 8
GR = 8192
ITERS = 3
SEGMENT_SPACING = 128
FRAME_TOTAL = 2048


def exponent_flat_draw(key, shape, lower, upper):
    return jnp.exp(jax.random.uniform(key, shape, jnp.float32, math.log(lower), math.log(upper)))


def draw_series(key, part):
    key = jax.random.fold_in(key, 101)
    disturbance_seed_handle, location_seed_handle, pulse_seed_handle, oscillation_seed_handle = jax.random.split(key, 4)
    wave_keys = jax.random.split(oscillation_seed_handle, 7)
    wave_count = 6
    noise_draw = jax.random.normal(disturbance_seed_handle, (FRAME_TOTAL, GX, GR), jnp.float32)
    point_scale = exponent_flat_draw(location_seed_handle, (GX, GR), 0.3, 3.0)
    magnitude_profile = exponent_flat_draw(pulse_seed_handle, (FRAME_TOTAL // SEGMENT_SPACING,), 0.5, 2.0)
    rising = 3.0
    strength = exponent_flat_draw(wave_keys[2], (wave_count,), 0.25, 0.7)
    segment_amp = exponent_flat_draw(wave_keys[3], (wave_count, FRAME_TOTAL // SEGMENT_SPACING), 0.4, 2.5)
    position = jnp.arange(GR, dtype=jnp.float32) / (GR - 1)
    point_scale = point_scale * jnp.power(rising, position)[None, :]
    magnitude_profile = jnp.repeat(magnitude_profile, SEGMENT_SPACING)
    total = noise_draw * magnitude_profile[:, None, None] * point_scale[None, :, :]
    wave_freq = jax.random.uniform(wave_keys[0], (wave_count,), jnp.float32, 2.0, NFFT / 2.0 - 2.0) / NFFT
    center = jax.random.uniform(wave_keys[1], (wave_count,), jnp.float32, 0.1, 0.9)
    wave_x = jax.random.randint(wave_keys[4], (wave_count,), 1, 4, jnp.int32).astype(jnp.float32)
    wave_r = jax.random.randint(wave_keys[5], (wave_count,), 2, 9, jnp.int32).astype(jnp.float32)
    jitter = jax.random.uniform(wave_keys[6], (wave_count, GX, GR), jnp.float32, -0.6, 0.6)
    snap_time = jnp.arange(FRAME_TOTAL, dtype=jnp.float32)
    x_place = jnp.arange(GX, dtype=jnp.float32) / GX
    for wave in range(wave_count):
        offset = (position - center[wave]) / 0.08
        bump = jnp.exp(-0.5 * offset * offset)
        amp_time = jnp.repeat(segment_amp[wave], SEGMENT_SPACING) * strength[wave]
        space_phase = 2.0 * math.pi * (wave_x[wave] * x_place[:, None] + wave_r[wave] * position[None, :]) + jitter[wave]
        cycles = jnp.mod(wave_freq[wave] * snap_time, 1.0)
        shape_space = bump[None, :] * point_scale
        total = total + amp_time[:, None, None] * shape_space[None, :, :] * jnp.cos(2.0 * math.pi * cycles[:, None, None] - space_phase[None, :, :])
    return total.astype(jnp.bfloat16)


def draw_block_start(key, part):
    key = jax.random.fold_in(key, 202)
    jitter = jax.random.randint(key, (BLOCKS,), -(SEGMENT_SPACING // 4), SEGMENT_SPACING // 4 + 1, jnp.int32)
    number = jnp.arange(BLOCKS, dtype=jnp.int32)
    inside = (number > 0) & (number < BLOCKS - 1)
    return number * SEGMENT_SPACING + jnp.where(inside, jitter, 0)


def draw_freq_index(key, part):
    key = jax.random.fold_in(key, 303)
    pick_key, order_key = jax.random.split(key)
    middle = jax.random.permutation(pick_key, NFFT // 2 - 1)[:NF - 2].astype(jnp.int32) + 1
    chosen = jnp.concatenate([jnp.array([0, NFFT // 2], dtype=jnp.int32), middle])
    return chosen[jax.random.permutation(order_key, NF)]


def setup_inputs(seed: int = 0, part: int = 0) -> dict:
    key_of = jax.random.split(jax.random.key(seed), 4)
    part_keys = jax.random.split(jax.random.fold_in(key_of[3], part), 4)
    return {
        "series": draw_series(jax.random.fold_in(jax.random.fold_in(key_of[3], part), 71), part),
        "block_start": draw_block_start(jax.random.fold_in(key_of[3], 71), part),
        "freq_index": draw_freq_index(jax.random.fold_in(key_of[3], 71), part),
    }


def dft_basis(freq_index, window_len):
    steps_int = jnp.arange(window_len, dtype=jnp.int32)
    phase_int = freq_index[:, None] * steps_int[None, :] % window_len
    angle = 2.0 * math.pi / window_len * phase_int.astype(jnp.float32)
    window = 0.5 - 0.5 * jnp.cos(2.0 * math.pi / window_len * steps_int.astype(jnp.float32))
    weighting = window / jnp.sqrt(jnp.sum(window * window))
    table = jnp.stack([jnp.cos(angle), -jnp.sin(angle)], axis=1) * weighting[None, None, :]
    return table.reshape(-1, window_len).astype(jnp.bfloat16)

def apply_cross(cross_real, cross_imag, vec_real, vec_imag):
    highest = lax.Precision.HIGHEST
    out_real = jnp.einsum('kbd,kd->kb', cross_real, vec_real, precision=highest) - jnp.einsum('kbd,kd->kb', cross_imag, vec_imag, precision=highest)
    out_imag = jnp.einsum('kbd,kd->kb', cross_real, vec_imag, precision=highest) + jnp.einsum('kbd,kd->kb', cross_imag, vec_real, precision=highest)
    return (out_real, out_imag)

def leading_vector(cross_real, cross_imag, sweeps):
    initial = jnp.full(cross_real.shape[:2], 1.0 / math.sqrt(cross_real.shape[1]), jnp.float32)
    vec_real = initial
    vec_imag = jnp.zeros_like(initial)
    for sweep_index in range(sweeps):
        out_real, out_imag = apply_cross(cross_real, cross_imag, vec_real, vec_imag)
        length = jnp.sqrt(lax.optimization_barrier(jnp.sum(out_real * out_real + out_imag * out_imag, axis=1, keepdims=True)))
        vec_real = out_real / length
        vec_imag = out_imag / length
    out_real, out_imag = apply_cross(cross_real, cross_imag, vec_real, vec_imag)
    spectrum = lax.optimization_barrier(jnp.sum(vec_real * out_real + vec_imag * out_imag, axis=1))
    return (vec_real, vec_imag, spectrum)

def reference(series, block_start, freq_index):
    snap_rows, slab_rows, plane = series.shape
    blocks = block_start.shape[0]
    retained = freq_index.shape[0]
    total_points = slab_rows * plane
    history = series.reshape(snap_rows, total_points)
    basis = dft_basis(freq_index, NFFT)

    def one_block(carried, offset):
        segment = lax.dynamic_slice_in_dim(history, offset, NFFT, 0)
        return (carried, jnp.dot(basis, segment, preferred_element_type=jnp.float32).astype(jnp.bfloat16))
    unused, tiles = lax.scan(one_block, jnp.int32(0), block_start)
    coefficients = tiles.reshape(blocks, retained, 2, slab_rows, plane)
    highest = lax.Precision.HIGHEST

    def gram_one(index):
        tile = lax.dynamic_index_in_dim(coefficients, index, 1, keepdims=False).astype(jnp.float32)
        product = jnp.einsum('bcxr,dexr->cebd', tile, tile, precision=highest)
        return (product[0, 0] + product[1, 1], product[0, 1] - product[1, 0])
    frequency_ids = jnp.arange(retained, dtype=jnp.int32)
    cross_real, cross_imag = lax.map(gram_one, frequency_ids)
    norm_scale = 1.0 / (blocks * total_points)
    cross_real = cross_real * norm_scale
    cross_imag = cross_imag * norm_scale
    vec_real, vec_imag, spectrum = leading_vector(cross_real, cross_imag, ITERS)
    low_real = vec_real.astype(jnp.bfloat16)
    low_imag = vec_imag.astype(jnp.bfloat16)

    def mode_one(index):
        tile = lax.dynamic_index_in_dim(coefficients, index, 1, keepdims=False).astype(jnp.float32)
        part_real = lax.dynamic_index_in_dim(low_real, index, 0, keepdims=False)
        part_imag = lax.dynamic_index_in_dim(low_imag, index, 0, keepdims=False)
        mixing = jnp.stack([jnp.stack([part_real, part_imag], axis=0), jnp.stack([-part_imag, part_real], axis=0)], axis=0).astype(jnp.float32)
        return jnp.einsum('bcxr,ceb->exr', tile, mixing, precision=highest)
    raw_stack = lax.map(mode_one, frequency_ids)
    raw_modes = jnp.transpose(raw_stack, (1, 0, 2, 3))
    energy = lax.optimization_barrier(jnp.sum(raw_modes[0] * raw_modes[0] + raw_modes[1] * raw_modes[1], axis=(1, 2))) / total_points
    modes = raw_modes * lax.rsqrt(energy + 1e-06)[None, :, None, None]
    return (modes, spectrum)
```

```python
import functools
import math

import jax
import jax.numpy as jnp
from jax import lax
from jax.experimental import pallas as pl
from jax.experimental.pallas import tpu as pltpu
from jax.sharding import PartitionSpec as P

NFFT = 256
ITERS = 3
SPACING = 128
JITTER = 32
SPAN = NFFT + 2 * JITTER
PACK = 8
AHEAD = 3
MESH = pl.DeviceIdType.MESH
F32 = jnp.float32
BF16 = jnp.bfloat16
HIGHEST = lax.Precision.HIGHEST


def dft_basis(freq_index, window_len):
    steps_int = jnp.arange(window_len, dtype=jnp.int32)
    phase_int = freq_index[:, None] * steps_int[None, :] % window_len
    angle = 2.0 * math.pi / window_len * phase_int.astype(F32)
    window = 0.5 - 0.5 * jnp.cos(2.0 * math.pi / window_len * steps_int.astype(F32))
    weighting = window / jnp.sqrt(jnp.sum(window * window))
    table = jnp.stack([jnp.cos(angle), -jnp.sin(angle)], axis=1) * weighting[None, None, :]
    return table.reshape(-1, window_len).astype(BF16)


def iota(shape, dim):
    return lax.broadcasted_iota(jnp.int32, shape, dim)


def exact_dot(a, b):
    return lax.dot_general(a, b, (((1,), (0,)), ((), ())), precision=HIGHEST, preferred_element_type=F32)


def kernel(
    cfg, start_ref, basis_ref, series_ref, modes_ref, spec_ref,
    hist, coef, moved, shifted, gram, packed, parts, total,
    own_sem, z_send, z_recv, x_send, x_recv, s_send, s_recv, g_send, g_recv,
):
    npts, nsub, nfreq, snaps, planes, width, cols, blocks, groups, share = cfg
    n = npts * nsub
    pieces = width // cols
    chunks = planes * pieces
    local = groups // nfreq
    rows = blocks * 2 * PACK
    length = n * snaps
    points = planes * nfreq * n * width
    me = lax.axis_index("pts") * nsub + lax.axis_index("sub")
    mine = lax.axis_index("freq")

    def z_device(i):
        other = lax.rem(me + i, n)
        return other, {"pts": other // nsub, "sub": lax.rem(other, nsub)}

    def x_device(i):
        other = lax.rem(mine + i, nfreq)
        return other, {"freq": other}

    barrier = pltpu.get_barrier_semaphore()

    @pl.loop(1, n)
    def _(i):
        pl.semaphore_signal(barrier, inc=1, device_id=z_device(i)[1], device_id_type=MESH)

    @pl.loop(1, nfreq)
    def _(i):
        pl.semaphore_signal(barrier, inc=1, device_id=x_device(i)[1], device_id_type=MESH)

    pl.semaphore_wait(barrier, n - 1 + nfreq - 1)

    def z_copy(c, i):
        other, where = z_device(i)
        at = pl.multiple_of(other * width + lax.rem(c, pieces) * cols, cols)
        return pltpu.make_async_remote_copy(
            src_ref=series_ref.at[c // pieces, :, pl.ds(at, cols)],
            dst_ref=hist.at[c, pl.ds(pl.multiple_of(me * snaps, snaps), snaps)],
            send_sem=z_send.at[c, i],
            recv_sem=z_recv.at[c, i],
            device_id=where,
            device_id_type=MESH,
        )

    def own_copy(c):
        at = pl.multiple_of(me * width + lax.rem(c, pieces) * cols, cols)
        return pltpu.make_async_copy(
            series_ref.at[c // pieces, :, pl.ds(at, cols)],
            hist.at[c, pl.ds(pl.multiple_of(me * snaps, snaps), snaps)],
            own_sem.at[c],
        )

    def x_copy(c, i):
        other, where = x_device(i)
        return pltpu.make_async_remote_copy(
            src_ref=coef.at[c, pl.ds(other * local, local)],
            dst_ref=moved.at[i - 1, c],
            send_sem=x_send.at[c, i],
            recv_sem=x_recv.at[c, i],
            device_id=where,
            device_id_type=MESH,
        )

    def z_start(c):
        @pl.loop(1, n)
        def _(i):
            z_copy(c, i).start()

        own_copy(c).start()

    ahead = min(AHEAD, chunks)
    for c in range(ahead):
        z_start(c)

    firsts = [min(max(SPACING * b - JITTER, 0), length - SPAN) for b in range(blocks)]
    gap = iota((NFFT, SPAN), 1) - iota((NFFT, SPAN), 0)
    for b in range(blocks):
        move = jnp.where(gap == start_ref[b] - firsts[b], 1.0, 0.0).astype(BF16)
        shifted[b] = jnp.dot(basis_ref[...], move, preferred_element_type=F32).astype(BF16)
    gram[...] = jnp.zeros_like(gram)

    def add_gram(g, tile):
        gram[g] += lax.dot_general(tile, tile, (((1,), (1,)), ((), ())), preferred_element_type=F32)

    def take_moved(c):
        @pl.loop(1, nfreq)
        def _(i):
            x_copy(c, i).wait_recv()
            for g in range(local):
                add_gram(g, moved[i - 1, c, g])

    @pl.loop(0, chunks)
    def _(c):
        @pl.when(c + ahead < chunks)
        def _():
            z_start(c + ahead)

        own_copy(c).wait()

        @pl.loop(1, n)
        def _(i):
            z_copy(c, i).wait_recv()

        for b in range(blocks):
            out = jnp.dot(shifted[b], hist[c, firsts[b] : firsts[b] + SPAN, :], preferred_element_type=F32)
            coef[c, :, b * 2 * PACK : (b + 1) * 2 * PACK, :] = out.astype(BF16).reshape(groups, 2 * PACK, cols)

        @pl.loop(1, nfreq)
        def _(i):
            x_copy(c, i).start()

        for g in range(local):
            add_gram(g, coef[c, mine * local + g])

        @pl.when(c > 0)
        def _():
            take_moved(c - 1)

    take_moved(chunks - 1)

    row, col = iota((rows, rows), 0), iota((rows, rows), 1)
    same = jnp.where((row // 2) % PACK == (col // 2) % PACK, 1.0, 0.0).astype(F32)
    eye = row == col
    turn = jnp.where(
        (row // 2 == col // 2) & (row != col), jnp.where(row % 2 == 0, -1.0, 1.0), 0.0
    ).astype(F32)
    lanes = packed.shape[1]
    slot_r, slot_l = iota((rows, lanes), 0), iota((rows, lanes), 1)
    place = slot_r // (2 * PACK) * 2 + slot_r % 2
    slots = 32

    def chooser(g):
        return jnp.where(slot_l == g * slots + place, 1.0, 0.0).astype(F32)

    packed[...] = jnp.zeros_like(packed)
    for g in range(local):
        packed[:rows, :] += exact_dot(gram[g] * same, chooser(g))

    def s_copy(i):
        other, where = z_device(i)
        return pltpu.make_async_remote_copy(
            src_ref=packed.at[pl.ds(pl.multiple_of(other * share, share), share)],
            dst_ref=parts.at[me],
            send_sem=s_send.at[i],
            recv_sem=s_recv.at[i],
            device_id=where,
            device_id_type=MESH,
        )

    def g_copy(i):
        here = pl.ds(pl.multiple_of(me * share, share), share)
        return pltpu.make_async_remote_copy(
            src_ref=total.at[here],
            dst_ref=total.at[here],
            send_sem=g_send.at[i],
            recv_sem=g_recv.at[i],
            device_id=z_device(i)[1],
            device_id_type=MESH,
        )

    here = pl.ds(pl.multiple_of(me * share, share), share)

    @pl.loop(1, n)
    def _(i):
        s_copy(i).start()

    parts[me] = packed[here, :]

    @pl.loop(1, n)
    def _(i):
        s_copy(i).wait()

    total[here, :] = jnp.sum(parts[...], axis=0)

    @pl.loop(1, n)
    def _(i):
        g_copy(i).start()

    @pl.loop(1, n)
    def _(i):
        g_copy(i).wait()

    scale = 1.0 / (blocks * points)
    head = jnp.where(iota((1, rows), 1) % 2 == 0, 1.0 / math.sqrt(blocks), 0.0).astype(F32)
    mode_r, mode_c = iota((2 * PACK, rows), 0), iota((2 * PACK, rows), 1)
    mode_same = mode_r % PACK == (mode_c // 2) % PACK
    mode_first = mode_c == (mode_r % PACK) * 2

    def over(mat, vec):
        return jnp.sum(mat * vec, axis=1, keepdims=True)

    def down(mat, vec):
        return jnp.sum(mat * vec, axis=0, keepdims=True)

    def upright(vec):
        return jnp.sum(jnp.where(eye, vec, 0.0), axis=1, keepdims=True)

    def flat(vec):
        return jnp.sum(jnp.where(eye, vec, 0.0), axis=0, keepdims=True)

    mixes, gains = [], []
    for g in range(local):
        choose = chooser(g)
        block = lax.dot_general(
            total[:rows, :], choose, (((1,), (1,)), ((), ())), precision=HIGHEST, preferred_element_type=F32
        ) * same
        both = (block - exact_dot(exact_dot(turn, block), turn)) * scale
        vec = head
        for _ in range(ITERS):
            out = over(both, vec)
            vec = flat(out) / jnp.sqrt(down(same, out * out))
        spec_ref[g : g + 1, :] = down(same, over(both, vec) * upright(vec))
        low_bf = vec.astype(BF16)
        low = low_bf.astype(F32)
        low_up = upright(low)
        energy = down(same, over(both, low) * low_up) * (points * blocks / points)
        gain = lax.rsqrt(energy + 1e-06)
        turned = flat(over(turn, low))
        mix = jnp.where(mode_same, jnp.where(mode_r < PACK, low, turned), 0.0)
        mixes.append(mix.astype(BF16))
        gains.append(jnp.sum(jnp.where(mode_first, gain, 0.0), axis=1, keepdims=True))

    @pl.loop(0, planes)
    def _(p):
        for q in range(pieces):
            c = p * pieces + q
            at = pl.ds(q * cols, cols)
            for g in range(local):
                modes_ref[mine * planes + p, pl.ds(g * 2 * PACK, 2 * PACK), at] = (
                    jnp.dot(mixes[g], coef[c, mine * local + g], preferred_element_type=F32) * gains[g]
                )
            for i in range(1, nfreq):
                source = lax.rem(mine + nfreq - i, nfreq)
                for g in range(local):
                    modes_ref[source * planes + p, pl.ds(g * 2 * PACK, 2 * PACK), at] = (
                        jnp.dot(mixes[g], moved[i - 1, c, g], preferred_element_type=F32) * gains[g]
                    )

    @pl.loop(0, chunks)
    def _(c):
        @pl.loop(1, n)
        def _(i):
            z_copy(c, i).wait_send()

        @pl.loop(1, nfreq)
        def _(i):
            x_copy(c, i).wait_send()


def shards(series, block_start, freq_index):
    snaps, planes, plane = series.shape
    npts, nsub, nfreq = (lax.axis_size(a) for a in ("pts", "sub", "freq"))
    n = npts * nsub
    width = plane // n
    cols = min(256, width)
    blocks = block_start.shape[0]
    retained = freq_index.shape[0]
    groups = retained // PACK
    local = groups // nfreq
    rows = blocks * 2 * PACK
    chunks = planes * (width // cols)
    share = -(-rows // (8 * n)) * 8
    lanes = max(128, local * 32)
    basis = dft_basis(freq_index, NFFT)
    turned = jnp.transpose(series, (1, 0, 2))
    cfg = (npts, nsub, nfreq, snaps, planes, width, cols, blocks, groups, share)
    dma = pltpu.SemaphoreType.DMA
    raw, spec = pl.pallas_call(
        functools.partial(kernel, cfg),
        out_shape=(
            jax.ShapeDtypeStruct((nfreq * planes, local * 2 * PACK, width), F32),
            jax.ShapeDtypeStruct((local, rows), F32),
        ),
        in_specs=[
            pl.BlockSpec(memory_space=pltpu.SMEM),
            pl.BlockSpec(memory_space=pltpu.VMEM),
            pl.BlockSpec(memory_space=pl.ANY),
        ],
        out_specs=(pl.BlockSpec(memory_space=pltpu.VMEM), pl.BlockSpec(memory_space=pltpu.VMEM)),
        scratch_shapes=[
            pltpu.VMEM((chunks, n * snaps, cols), BF16),
            pltpu.VMEM((chunks, groups, rows, cols), BF16),
            pltpu.VMEM((nfreq - 1, chunks, local, rows, cols), BF16),
            pltpu.VMEM((blocks, 2 * retained, SPAN), BF16),
            pltpu.VMEM((local, rows, rows), F32),
            pltpu.VMEM((n * share, lanes), F32),
            pltpu.VMEM((n, share, lanes), F32),
            pltpu.VMEM((n * share, lanes), F32),
            dma((chunks,)),
            dma((chunks, n)),
            dma((chunks, n)),
            dma((chunks, nfreq)),
            dma((chunks, nfreq)),
            dma((n,)),
            dma((n,)),
            dma((n,)),
            dma((n,)),
        ],
        compiler_params=pltpu.CompilerParams(
            collective_id=0, has_side_effects=True, vmem_limit_bytes=60 * 1024 * 1024
        ),
    )(block_start, basis, turned)
    modes = raw.reshape(nfreq * planes, local, 2, PACK, width).transpose(2, 1, 3, 0, 4)
    modes = modes.reshape(2, local * PACK, nfreq * planes, width)
    return modes, spec[:, : 2 * PACK : 2].reshape(local * PACK)


def solution(mesh):
    in_specs = (P(("pts", "sub"), "freq", "groups"), P(), P())
    out_specs = (P(None, "freq", "groups", ("pts", "sub")), P(("groups", "freq")))
    return jax.shard_map(shards, mesh=mesh, in_specs=in_specs, out_specs=out_specs, check_vma=False)
```

```python
import functools
import math

import jax
import jax.numpy as jnp
from jax import lax
from jax.experimental import pallas as pl
from jax.experimental.pallas import tpu as pltpu
from jax.sharding import PartitionSpec as P

NFFT = 256
ITERS = 3
SPACING = 128
JITTER = 32
SPAN = NFFT + 2 * JITTER
PACK = 8
MESH = pl.DeviceIdType.MESH
F32 = jnp.float32
BF16 = jnp.bfloat16
HIGHEST = lax.Precision.HIGHEST


def dft_basis(freq_ref, retained):
    shape = (2 * retained, NFFT)
    row, step = iota(shape, 0), iota(shape, 1)
    freq = lax.fori_loop(
        0, retained, lambda j, held: jnp.where(row // 2 == j, freq_ref[j], held), jnp.zeros(shape, jnp.int32)
    )
    turn = 2.0 * math.pi / NFFT
    angle = turn * (freq * step % NFFT).astype(F32)
    window = 0.5 - 0.5 * jnp.cos(turn * iota((1, NFFT), 1).astype(F32))
    weighting = window / jnp.sqrt(jnp.sum(window * window))
    return (jnp.where(row % 2 == 0, jnp.cos(angle), -jnp.sin(angle)) * weighting).astype(BF16)


def iota(shape, dim):
    return lax.broadcasted_iota(jnp.int32, shape, dim)


def exact_dot(a, b):
    return lax.dot_general(a, b, (((1,), (0,)), ((), ())), precision=HIGHEST, preferred_element_type=F32)


def kernel(
    cfg, start_ref, freq_ref, series_ref, modes_ref, spec_ref,
    taken, stage, hist, coef, moved, shifted, gram, packed, parts, total,
    load_sem, z_send, z_recv, x_send, x_recv, s_send, s_recv, g_send, g_recv,
):
    npts, nsub, nfreq, snaps, planes, width, cols, blocks, groups, share = cfg
    n = npts * nsub
    pieces = width // cols
    chunks = planes * pieces
    local = groups // nfreq
    rows = blocks * 2 * PACK
    length = n * snaps
    points = planes * nfreq * n * width
    me = lax.axis_index("pts") * nsub + lax.axis_index("sub")
    mine = lax.axis_index("freq")

    def z_device(i):
        other = lax.rem(me + i, n)
        return other, {"pts": other // nsub, "sub": lax.rem(other, nsub)}

    def x_device(i):
        other = lax.rem(mine + i, nfreq)
        return other, {"freq": other}

    barrier = pltpu.get_barrier_semaphore()

    @pl.loop(1, n)
    def _(i):
        pl.semaphore_signal(barrier, inc=1, device_id=z_device(i)[1], device_id_type=MESH)

    @pl.loop(1, nfreq)
    def _(i):
        pl.semaphore_signal(barrier, inc=1, device_id=x_device(i)[1], device_id_type=MESH)

    pl.semaphore_wait(barrier, n - 1 + nfreq - 1)

    own_rows = pl.ds(pl.multiple_of(me * snaps, snaps), snaps)

    def z_copy(c, i):
        return pltpu.make_async_remote_copy(
            src_ref=stage.at[lax.rem(c // planes, 2), i - 1, lax.rem(c, planes)],
            dst_ref=hist.at[c, own_rows],
            send_sem=z_send.at[c, i],
            recv_sem=z_recv.at[c, i],
            device_id=z_device(i)[1],
            device_id_type=MESH,
        )

    def load(q, k):
        at = pl.multiple_of(lax.rem(me + k + 1, n) * width + q * cols, cols)
        slot = lax.rem(k, 2)
        return pltpu.make_async_copy(series_ref.at[:, :, pl.ds(at, cols)], taken.at[slot], load_sem.at[slot])

    def regroup(q, send):
        load(q, 0).start()

        @pl.loop(0, n)
        def _(k):
            @pl.when(k + 1 < n)
            def _():
                load(q, k + 1).start()

            load(q, k).wait()
            tile = jnp.swapaxes(taken[lax.rem(k, 2)], 0, 1)

            @pl.when(k + 1 < n)
            def _():
                stage[lax.rem(q, 2), k] = tile
                if send:
                    z_copy(q * planes, k + 1).start()

            @pl.when(k + 1 == n)
            def _():
                hist[pl.ds(q * planes, planes), own_rows, :] = tile

    def z_sent(q):
        @pl.loop(0, planes)
        def _(p):
            @pl.loop(1, n)
            def _(i):
                z_copy(q * planes + p, i).wait_send()

    def x_copy(c, i):
        other, where = x_device(i)
        return pltpu.make_async_remote_copy(
            src_ref=coef.at[c, pl.ds(other * local, local)],
            dst_ref=moved.at[i - 1, c],
            send_sem=x_send.at[c, i],
            recv_sem=x_recv.at[c, i],
            device_id=where,
            device_id_type=MESH,
        )

    def z_start(c):
        @pl.loop(1, n)
        def _(i):
            z_copy(c, i).start()

    regroup(0, True)
    ahead = planes - 1
    for c in range(1, ahead):
        z_start(c)

    firsts = [min(max(SPACING * b - JITTER, 0), length - SPAN) for b in range(blocks)]
    gap = iota((NFFT, SPAN), 1) - iota((NFFT, SPAN), 0)
    basis = dft_basis(freq_ref, groups * PACK)
    for b in range(blocks):
        move = jnp.where(gap == start_ref[b] - firsts[b], 1.0, 0.0).astype(BF16)
        shifted[b] = jnp.dot(basis, move, preferred_element_type=F32).astype(BF16)
    gram[...] = jnp.zeros_like(gram)

    def add_gram(g, tile):
        gram[g] += lax.dot_general(tile, tile, (((1,), (1,)), ((), ())), preferred_element_type=F32)

    def take_moved(c):
        @pl.loop(1, nfreq)
        def _(i):
            x_copy(c, i).wait_recv()
            for g in range(local):
                add_gram(g, moved[i - 1, c, g])

    @pl.loop(0, chunks)
    def _(c):
        @pl.when(c + ahead < chunks)
        def _():
            z_start(c + ahead)

        @pl.when((lax.rem(c, planes) == 0) & (c + planes < chunks))
        def _():
            q = c // planes + 1

            @pl.when(q > 1)
            def _():
                z_sent(q - 2)

            regroup(q, False)

        @pl.loop(1, n)
        def _(i):
            z_copy(c, i).wait_recv()

        for b in range(blocks):
            out = jnp.dot(shifted[b], hist[c, firsts[b] : firsts[b] + SPAN, :], preferred_element_type=F32)
            coef[c, :, b * 2 * PACK : (b + 1) * 2 * PACK, :] = out.astype(BF16).reshape(groups, 2 * PACK, cols)

        @pl.loop(1, nfreq)
        def _(i):
            x_copy(c, i).start()

        for g in range(local):
            add_gram(g, coef[c, mine * local + g])

        @pl.when(c > 0)
        def _():
            take_moved(c - 1)

    take_moved(chunks - 1)

    row, col = iota((rows, rows), 0), iota((rows, rows), 1)
    same = jnp.where((row // 2) % PACK == (col // 2) % PACK, 1.0, 0.0).astype(F32)
    eye = row == col
    turn = jnp.where(
        (row // 2 == col // 2) & (row != col), jnp.where(row % 2 == 0, -1.0, 1.0), 0.0
    ).astype(F32)
    lanes = packed.shape[1]
    slot_r, slot_l = iota((rows, lanes), 0), iota((rows, lanes), 1)
    place = slot_r // (2 * PACK) * 2 + slot_r % 2
    slots = 32

    def chooser(g):
        return jnp.where(slot_l == g * slots + place, 1.0, 0.0).astype(F32)

    packed[...] = jnp.zeros_like(packed)
    for g in range(local):
        packed[:rows, :] += exact_dot(gram[g] * same, chooser(g))

    def s_copy(i):
        other, where = z_device(i)
        return pltpu.make_async_remote_copy(
            src_ref=packed.at[pl.ds(pl.multiple_of(other * share, share), share)],
            dst_ref=parts.at[me],
            send_sem=s_send.at[i],
            recv_sem=s_recv.at[i],
            device_id=where,
            device_id_type=MESH,
        )

    def g_copy(i):
        here = pl.ds(pl.multiple_of(me * share, share), share)
        return pltpu.make_async_remote_copy(
            src_ref=total.at[here],
            dst_ref=total.at[here],
            send_sem=g_send.at[i],
            recv_sem=g_recv.at[i],
            device_id=z_device(i)[1],
            device_id_type=MESH,
        )

    here = pl.ds(pl.multiple_of(me * share, share), share)

    @pl.loop(1, n)
    def _(i):
        s_copy(i).start()

    parts[me] = packed[here, :]

    @pl.loop(1, n)
    def _(i):
        s_copy(i).wait()

    total[here, :] = jnp.sum(parts[...], axis=0)

    @pl.loop(1, n)
    def _(i):
        g_copy(i).start()

    @pl.loop(1, n)
    def _(i):
        g_copy(i).wait()

    scale = 1.0 / (blocks * points)
    head = jnp.where(iota((1, rows), 1) % 2 == 0, 1.0 / math.sqrt(blocks), 0.0).astype(F32)
    mode_r, mode_c = iota((2 * PACK, rows), 0), iota((2 * PACK, rows), 1)
    mode_same = mode_r % PACK == (mode_c // 2) % PACK
    mode_first = mode_c == (mode_r % PACK) * 2

    def over(mat, vec):
        return jnp.sum(mat * vec, axis=1, keepdims=True)

    def down(mat, vec):
        return jnp.sum(mat * vec, axis=0, keepdims=True)

    def upright(vec):
        return jnp.sum(jnp.where(eye, vec, 0.0), axis=1, keepdims=True)

    def flat(vec):
        return jnp.sum(jnp.where(eye, vec, 0.0), axis=0, keepdims=True)

    mixes, gains = [], []
    spec = jnp.zeros((1, lanes), F32)
    for g in range(local):
        choose = chooser(g)
        block = lax.dot_general(
            total[:rows, :], choose, (((1,), (1,)), ((), ())), precision=HIGHEST, preferred_element_type=F32
        ) * same
        both = (block - exact_dot(exact_dot(turn, block), turn)) * scale
        vec = head
        for _ in range(ITERS):
            out = over(both, vec)
            vec = flat(out) / jnp.sqrt(down(same, out * out))
        values = down(same, over(both, vec) * upright(vec))
        slot = (slot_r % 2 == 0) & (slot_r < 2 * PACK) & (slot_l == g * PACK + slot_r // 2)
        spec += down(jnp.where(slot, 1.0, 0.0), upright(values))
        low_bf = vec.astype(BF16)
        low = low_bf.astype(F32)
        low_up = upright(low)
        energy = down(same, over(both, low) * low_up) * (points * blocks / points)
        gain = lax.rsqrt(energy + 1e-06)
        turned = flat(over(turn, low))
        mix = jnp.where(mode_same, jnp.where(mode_r < PACK, low, turned), 0.0)
        mixes.append(mix.astype(BF16))
        gains.append(jnp.sum(jnp.where(mode_first, gain, 0.0), axis=1, keepdims=True))

    spec_ref[...] = spec

    @pl.loop(0, planes)
    def _(p):
        for q in range(pieces):
            c = q * planes + p
            at = pl.ds(q * cols, cols)
            for g in range(local):
                modes_ref[mine * planes + p, pl.ds(g * 2 * PACK, 2 * PACK), at] = (
                    jnp.dot(mixes[g], coef[c, mine * local + g], preferred_element_type=F32) * gains[g]
                )
            for i in range(1, nfreq):
                source = lax.rem(mine + nfreq - i, nfreq)
                for g in range(local):
                    modes_ref[source * planes + p, pl.ds(g * 2 * PACK, 2 * PACK), at] = (
                        jnp.dot(mixes[g], moved[i - 1, c, g], preferred_element_type=F32) * gains[g]
                    )

    @pl.loop(0, chunks)
    def _(c):
        @pl.loop(1, nfreq)
        def _(i):
            x_copy(c, i).wait_send()

    for q in range(max(0, pieces - 2), pieces):
        z_sent(q)


def shards(series, block_start, freq_index):
    snaps, planes, plane = series.shape
    npts, nsub, nfreq = (lax.axis_size(a) for a in ("pts", "sub", "freq"))
    n = npts * nsub
    width = plane // n
    cols = min(256, width)
    blocks = block_start.shape[0]
    retained = freq_index.shape[0]
    groups = retained // PACK
    local = groups // nfreq
    rows = blocks * 2 * PACK
    chunks = planes * (width // cols)
    share = -(-rows // (8 * n)) * 8
    lanes = max(128, local * 32)
    cfg = (npts, nsub, nfreq, snaps, planes, width, cols, blocks, groups, share)
    dma = pltpu.SemaphoreType.DMA
    raw, spec = pl.pallas_call(
        functools.partial(kernel, cfg),
        out_shape=(
            jax.ShapeDtypeStruct((nfreq * planes, local * 2 * PACK, width), F32),
            jax.ShapeDtypeStruct((1, lanes), F32),
        ),
        in_specs=[
            pl.BlockSpec(memory_space=pltpu.SMEM),
            pl.BlockSpec(memory_space=pltpu.SMEM),
            pl.BlockSpec(memory_space=pl.ANY),
        ],
        out_specs=(pl.BlockSpec(memory_space=pltpu.VMEM), pl.BlockSpec(memory_space=pltpu.VMEM)),
        scratch_shapes=[
            pltpu.VMEM((2, snaps, planes, cols), BF16),
            pltpu.VMEM((min(2, width // cols), n - 1, planes, snaps, cols), BF16),
            pltpu.VMEM((chunks, n * snaps, cols), BF16),
            pltpu.VMEM((chunks, groups, rows, cols), BF16),
            pltpu.VMEM((nfreq - 1, chunks, local, rows, cols), BF16),
            pltpu.VMEM((blocks, 2 * retained, SPAN), BF16),
            pltpu.VMEM((local, rows, rows), F32),
            pltpu.VMEM((n * share, lanes), F32),
            pltpu.VMEM((n, share, lanes), F32),
            pltpu.VMEM((n * share, lanes), F32),
            dma((2,)),
            dma((chunks, n)),
            dma((chunks, n)),
            dma((chunks, nfreq)),
            dma((chunks, nfreq)),
            dma((n,)),
            dma((n,)),
            dma((n,)),
            dma((n,)),
        ],
        compiler_params=pltpu.CompilerParams(
            collective_id=0, has_side_effects=True, vmem_limit_bytes=60 * 1024 * 1024
        ),
    )(block_start, freq_index, series)
    modes = raw.reshape(nfreq * planes, local, 2, PACK, width).transpose(2, 1, 3, 0, 4)
    modes = modes.reshape(2, local * PACK, nfreq * planes, width)
    return modes, spec[0, : local * PACK]


def solution(mesh):
    in_specs = (P(("pts", "sub"), "freq", "groups"), P(), P())
    out_specs = (P(None, "freq", "groups", ("pts", "sub")), P(("groups", "freq")))
    return jax.shard_map(shards, mesh=mesh, in_specs=in_specs, out_specs=out_specs, check_vma=False)
```

```python
import functools
import math

import jax
import jax.numpy as jnp
from jax import lax
from jax.experimental import pallas as pl
from jax.experimental.pallas import tpu as pltpu
from jax.sharding import PartitionSpec as P

NFFT = 256
ITERS = 3
SPACING = 128
JITTER = 32
SPAN = NFFT + 2 * JITTER
PACK = 8
MESH = pl.DeviceIdType.MESH
F32 = jnp.float32
BF16 = jnp.bfloat16
HIGHEST = lax.Precision.HIGHEST


def dft_basis(freq_ref, retained):
    shape = (2 * retained, NFFT)
    row, step = iota(shape, 0), iota(shape, 1)
    freq = lax.fori_loop(
        0, retained, lambda j, held: jnp.where(row // 2 == j, freq_ref[j], held), jnp.zeros(shape, jnp.int32)
    )
    turn = 2.0 * math.pi / NFFT
    angle = turn * (freq * step % NFFT).astype(F32)
    window = 0.5 - 0.5 * jnp.cos(turn * iota((1, NFFT), 1).astype(F32))
    weighting = window / jnp.sqrt(jnp.sum(window * window))
    return (jnp.where(row % 2 == 0, jnp.cos(angle), -jnp.sin(angle)) * weighting).astype(BF16)


def iota(shape, dim):
    return lax.broadcasted_iota(jnp.int32, shape, dim)


def exact_dot(a, b):
    return lax.dot_general(a, b, (((1,), (0,)), ((), ())), precision=HIGHEST, preferred_element_type=F32)


def kernel(
    cfg, start_ref, freq_ref, series_ref, modes_ref, spec_ref,
    taken, stage, hist, coef, moved, shifted, gram, packed, parts, total, turning,
    load_sem, z_send, z_recv, x_send, x_recv, s_send, s_recv, g_send, g_recv,
):
    npts, nsub, nfreq, snaps, planes, width, part, cols, blocks, groups, share = cfg
    n = npts * nsub
    pieces = width // part
    fold = cols // part
    chunks = planes * pieces
    local = groups // nfreq
    rows = blocks * 2 * PACK
    length = n * snaps
    points = planes * nfreq * n * width
    me = lax.axis_index("pts") * nsub + lax.axis_index("sub")
    mine = lax.axis_index("freq")

    def z_device(i):
        other = lax.rem(me + i, n)
        return other, {"pts": other // nsub, "sub": lax.rem(other, nsub)}

    def x_device(i):
        other = lax.rem(mine + i, nfreq)
        return other, {"freq": other}

    barrier = pltpu.get_barrier_semaphore()

    @pl.loop(1, n)
    def _(i):
        pl.semaphore_signal(barrier, inc=1, device_id=z_device(i)[1], device_id_type=MESH)

    @pl.loop(1, nfreq)
    def _(i):
        pl.semaphore_signal(barrier, inc=1, device_id=x_device(i)[1], device_id_type=MESH)

    pl.semaphore_wait(barrier, n - 1 + nfreq - 1)

    own_rows = pl.ds(pl.multiple_of(me * snaps, snaps), snaps)

    def z_copy(c, i):
        return pltpu.make_async_remote_copy(
            src_ref=stage.at[lax.rem(c // planes, 2), i - 1, lax.rem(c, planes)],
            dst_ref=hist.at[c, own_rows],
            send_sem=z_send.at[c, i],
            recv_sem=z_recv.at[c, i],
            device_id=z_device(i)[1],
            device_id_type=MESH,
        )

    def load(q, k):
        at = pl.multiple_of(lax.rem(me + k + 1, n) * width + q * part, part)
        slot = lax.rem(k, 2)
        return pltpu.make_async_copy(series_ref.at[:, :, pl.ds(at, part)], taken.at[slot], load_sem.at[slot])

    def regroup(q, send):
        load(q, 0).start()

        @pl.loop(0, n)
        def _(k):
            @pl.when(k + 1 < n)
            def _():
                load(q, k + 1).start()

            load(q, k).wait()
            tile = jnp.swapaxes(taken[lax.rem(k, 2)], 0, 1)

            @pl.when(k + 1 < n)
            def _():
                stage[lax.rem(q, 2), k] = tile
                if send:
                    z_copy(q * planes, k + 1).start()

            @pl.when(k + 1 == n)
            def _():
                hist[pl.ds(q * planes, planes), own_rows, :] = tile

    def z_sent(q):
        @pl.loop(0, planes)
        def _(p):
            @pl.loop(1, n)
            def _(i):
                z_copy(q * planes + p, i).wait_send()

    def spot(c):
        q = c // planes
        at = pl.multiple_of(lax.rem(q, fold) * part, part)
        return q // fold * planes + lax.rem(c, planes), pl.ds(at, part)

    def x_copy(c, i):
        other, where = x_device(i)
        wide, at = spot(c)
        return pltpu.make_async_remote_copy(
            src_ref=coef.at[wide, pl.ds(other * local, local), :, at],
            dst_ref=moved.at[i - 1, wide, :, :, at],
            send_sem=x_send.at[c, i],
            recv_sem=x_recv.at[c, i],
            device_id=where,
            device_id_type=MESH,
        )

    def z_start(c):
        @pl.loop(1, n)
        def _(i):
            z_copy(c, i).start()

    regroup(0, True)
    ahead = planes - 1
    for c in range(1, ahead):
        z_start(c)

    firsts = [min(max(SPACING * b - JITTER, 0), length - SPAN) for b in range(blocks)]
    gap = iota((NFFT, SPAN), 1) - iota((NFFT, SPAN), 0)
    basis = dft_basis(freq_ref, groups * PACK)
    for b in range(blocks):
        move = jnp.where(gap == start_ref[b] - firsts[b], 1.0, 0.0).astype(BF16)
        shifted[b] = jnp.dot(basis, move, preferred_element_type=F32).astype(BF16)
    gram[...] = jnp.zeros_like(gram)

    def add_gram(g, tile):
        gram[g] += lax.dot_general(tile, tile, (((1,), (1,)), ((), ())), preferred_element_type=F32)

    def take_moved(c):
        wide, at = spot(c)

        @pl.loop(1, nfreq)
        def _(i):
            x_copy(c, i).wait_recv()
            for g in range(local):
                add_gram(g, moved[i - 1, wide, g, :, at])

    @pl.loop(0, chunks)
    def _(c):
        @pl.when(c + ahead < chunks)
        def _():
            z_start(c + ahead)

        @pl.when((lax.rem(c, planes) == 0) & (c + planes < chunks))
        def _():
            q = c // planes + 1

            @pl.when(q > 1)
            def _():
                z_sent(q - 2)

            regroup(q, False)

        @pl.loop(1, n)
        def _(i):
            z_copy(c, i).wait_recv()

        wide, at = spot(c)
        for b in range(blocks):
            out = jnp.dot(shifted[b], hist[c, firsts[b] : firsts[b] + SPAN, :], preferred_element_type=F32)
            coef[wide, :, b * 2 * PACK : (b + 1) * 2 * PACK, at] = out.astype(BF16).reshape(groups, 2 * PACK, part)

        @pl.loop(1, nfreq)
        def _(i):
            x_copy(c, i).start()

        for g in range(local):
            add_gram(g, coef[wide, mine * local + g, :, at])

        @pl.when(c > 0)
        def _():
            take_moved(c - 1)

    take_moved(chunks - 1)

    row, col = iota((rows, rows), 0), iota((rows, rows), 1)
    same = jnp.where((row // 2) % PACK == (col // 2) % PACK, 1.0, 0.0).astype(F32)
    eye = row == col
    turn = jnp.where(
        (row // 2 == col // 2) & (row != col), jnp.where(row % 2 == 0, -1.0, 1.0), 0.0
    ).astype(F32)
    lanes = packed.shape[1]
    slot_r, slot_l = iota((rows, lanes), 0), iota((rows, lanes), 1)
    place = slot_r // (2 * PACK) * 2 + slot_r % 2
    slots = 32

    def chooser(g):
        return jnp.where(slot_l == g * slots + place, 1.0, 0.0).astype(F32)

    packed[...] = jnp.zeros_like(packed)
    for g in range(local):
        packed[:rows, :] += exact_dot(gram[g] * same, chooser(g))

    def s_copy(i):
        other, where = z_device(i)
        return pltpu.make_async_remote_copy(
            src_ref=packed.at[pl.ds(pl.multiple_of(other * share, share), share)],
            dst_ref=parts.at[me],
            send_sem=s_send.at[i],
            recv_sem=s_recv.at[i],
            device_id=where,
            device_id_type=MESH,
        )

    def g_copy(i):
        here = pl.ds(pl.multiple_of(me * share, share), share)
        return pltpu.make_async_remote_copy(
            src_ref=total.at[here],
            dst_ref=total.at[here],
            send_sem=g_send.at[i],
            recv_sem=g_recv.at[i],
            device_id=z_device(i)[1],
            device_id_type=MESH,
        )

    here = pl.ds(pl.multiple_of(me * share, share), share)

    @pl.loop(1, n)
    def _(i):
        s_copy(i).start()

    parts[me] = packed[here, :]

    @pl.loop(1, n)
    def _(i):
        s_copy(i).wait()

    total[here, :] = jnp.sum(parts[...], axis=0)

    @pl.loop(1, n)
    def _(i):
        g_copy(i).start()

    @pl.loop(1, n)
    def _(i):
        g_copy(i).wait()

    scale = 1.0 / (blocks * points)
    head = jnp.where(iota((1, rows), 1) % 2 == 0, 1.0 / math.sqrt(blocks), 0.0).astype(F32)
    mode_r, mode_c = iota((2 * PACK, rows), 0), iota((2 * PACK, rows), 1)
    mode_same = mode_r % PACK == (mode_c // 2) % PACK
    mode_first = mode_c == (mode_r % PACK) * 2

    def over(mat, vec):
        return jnp.sum(mat * vec, axis=1, keepdims=True)

    def down(mat, vec):
        return jnp.sum(mat * vec, axis=0, keepdims=True)

    def upright(vec):
        return jnp.sum(jnp.where(eye, vec, 0.0), axis=1, keepdims=True)

    def flat(vec):
        return jnp.sum(jnp.where(eye, vec, 0.0), axis=0, keepdims=True)

    every = range(local)
    chosen = [chooser(g) for g in every]
    summed = total[:rows, :]
    compact = [
        lax.dot_general(summed, chosen[g], (((1,), (1,)), ((), ())), precision=HIGHEST, preferred_element_type=F32)
        * same
        for g in every
    ]
    half = [exact_dot(turn, compact[g]) for g in every]
    cross = [(compact[g] - exact_dot(half[g], turn)) * scale for g in every]
    vecs = [head for g in every]
    for _ in range(ITERS):
        outs = [over(cross[g], vecs[g]) for g in every]
        sizes = [down(same, outs[g] * outs[g]) for g in every]
        vecs = [flat(outs[g]) / jnp.sqrt(sizes[g]) for g in every]
    lows = [vecs[g].astype(BF16).astype(F32) for g in every]
    ups = [upright(lows[g]) for g in every]
    energy = [down(same, over(cross[g], lows[g]) * ups[g]) * blocks for g in every]
    turned = [flat(over(turn, lows[g])) for g in every]
    gains = [
        jnp.sum(jnp.where(mode_first, lax.rsqrt(energy[g] + 1e-06), 0.0), axis=1, keepdims=True) for g in every
    ]
    mixes = [
        jnp.where(mode_same, jnp.where(mode_r < PACK, lows[g], turned[g]), 0.0).astype(BF16) for g in every
    ]
    values = [down(same, over(cross[g], vecs[g]) * upright(vecs[g])) for g in every]
    spec = jnp.zeros((1, lanes), F32)
    for g in every:
        slot = (slot_r % 2 == 0) & (slot_r < 2 * PACK) & (slot_l == g * PACK + slot_r // 2)
        spec += down(jnp.where(slot, 1.0, 0.0), upright(values[g]))
    spec_ref[...] = spec

    @pl.loop(0, width // cols)
    def _(q):
        at = pl.ds(pl.multiple_of(q * cols, cols), cols)
        for g in every:
            for p in range(planes):
                turning[g, mine * planes + p] = (
                    jnp.dot(mixes[g], coef[q * planes + p, mine * local + g], preferred_element_type=F32) * gains[g]
                )
                for i in range(1, nfreq):
                    source = lax.rem(mine + nfreq - i, nfreq)
                    turning[g, source * planes + p] = (
                        jnp.dot(mixes[g], moved[i - 1, q * planes + p, g], preferred_element_type=F32) * gains[g]
                    )
        for g in every:
            tile = jnp.swapaxes(turning[g], 0, 1)
            modes_ref[0, g * PACK : (g + 1) * PACK, :, at] = tile[:PACK]
            modes_ref[1, g * PACK : (g + 1) * PACK, :, at] = tile[PACK:]

    @pl.loop(0, chunks)
    def _(c):
        @pl.loop(1, nfreq)
        def _(i):
            x_copy(c, i).wait_send()

    for q in range(max(0, pieces - 2), pieces):
        z_sent(q)


def shards(series, block_start, freq_index):
    snaps, planes, plane = series.shape
    npts, nsub, nfreq = (lax.axis_size(a) for a in ("pts", "sub", "freq"))
    n = npts * nsub
    width = plane // n
    cols = min(256, width)
    part = min(128, width)
    blocks = block_start.shape[0]
    retained = freq_index.shape[0]
    groups = retained // PACK
    local = groups // nfreq
    rows = blocks * 2 * PACK
    chunks = planes * (width // part)
    wides = planes * (width // cols)
    share = -(-rows // (8 * n)) * 8
    lanes = max(128, local * 32)
    cfg = (npts, nsub, nfreq, snaps, planes, width, part, cols, blocks, groups, share)
    dma = pltpu.SemaphoreType.DMA
    modes, spec = pl.pallas_call(
        functools.partial(kernel, cfg),
        out_shape=(
            jax.ShapeDtypeStruct((2, local * PACK, nfreq * planes, width), F32),
            jax.ShapeDtypeStruct((1, lanes), F32),
        ),
        in_specs=[
            pl.BlockSpec(memory_space=pltpu.SMEM),
            pl.BlockSpec(memory_space=pltpu.SMEM),
            pl.BlockSpec(memory_space=pl.ANY),
        ],
        out_specs=(pl.BlockSpec(memory_space=pltpu.VMEM), pl.BlockSpec(memory_space=pltpu.VMEM)),
        scratch_shapes=[
            pltpu.VMEM((2, snaps, planes, part), BF16),
            pltpu.VMEM((min(2, width // part), n - 1, planes, snaps, part), BF16),
            pltpu.VMEM((chunks, n * snaps, part), BF16),
            pltpu.VMEM((wides, groups, rows, cols), BF16),
            pltpu.VMEM((nfreq - 1, wides, local, rows, cols), BF16),
            pltpu.VMEM((blocks, 2 * retained, SPAN), BF16),
            pltpu.VMEM((local, rows, rows), F32),
            pltpu.VMEM((n * share, lanes), F32),
            pltpu.VMEM((n, share, lanes), F32),
            pltpu.VMEM((n * share, lanes), F32),
            pltpu.VMEM((local, nfreq * planes, 2 * PACK, cols), F32),
            dma((2,)),
            dma((chunks, n)),
            dma((chunks, n)),
            dma((chunks, nfreq)),
            dma((chunks, nfreq)),
            dma((n,)),
            dma((n,)),
            dma((n,)),
            dma((n,)),
        ],
        compiler_params=pltpu.CompilerParams(
            collective_id=0, has_side_effects=True, vmem_limit_bytes=60 * 1024 * 1024
        ),
    )(block_start, freq_index, series)
    return modes, spec[0, : local * PACK]


def solution(mesh):
    in_specs = (P(("pts", "sub"), "freq", "groups"), P(), P())
    out_specs = (P(None, "freq", "groups", ("pts", "sub")), P(("groups", "freq")))
    return jax.shard_map(shards, mesh=mesh, in_specs=in_specs, out_specs=out_specs, check_vma=False)
```
